256 devices in a mesh: src: 16 (over x_lo, y, core), tgt: 16 (over x_hi, z).
Axes of the slice: x: 4 (x_hi: 2, x_lo: 2; x = x_hi * 2 + x_lo), y: 4, z: 8, core: 2. Of those that a mesh axis runs over, the one named last changes fastest.
Arguments:
- src_coords: float32 [3, 98304], P(None, 'src'), may hold values from 0 to 1, as said below
- tgt_coords: float32 [3, 98304], P(None, 'tgt'), may hold values from 0 to 1
- src_scaling: float32 [32, 98304], P('tgt', 'src'), may hold values from 0.25 to 4
- src_mass: float32 [32, 98304], P('tgt', 'src'), may hold values from 0.25 to 4
- tgt_mass: float32 [32, 98304], P(None, 'tgt'), may hold values from 0.25 to 4
Outputs:
- new_src_scaling: float32 [32, 98304], P('tgt', 'src')
- tgt_scaling: float32 [32, 98304], P('src', 'tgt')
The draws below stay inside these ranges and needn't reach their ends.
Inputs may be any that keep to these rules, and one draw needn't show every extreme that they name: `src_coords`: source points lie in the unit cube.
All inputs are finite; a program needn't handle non-finite values.
Results may differ from the reference program's by a relative error of at most 0.00036.
Values may be sent and summed in bfloat16 or wider, within the bound.
A program may use at most 64 MiB of HBM per device.

```python
import math
import jax
import jax.numpy as jnp
from jax import lax

WEIGHTS = 32
NS = 98304
NT = 98304


def draw_src_coords(key, part):
    base = jax.random.uniform(key, (3, NS), jnp.float32)
    first = 0.6 * base[0:1]
    return jnp.concatenate([first, base[1:]], axis=0)


def steps_of(stream_key, dims, shards, least, high):
    factor_of, own = 1.0, jax.random.fold_in(stream_key, 6)
    for axis_at, shards_of in shards:
        draws = jnp.exp(jax.random.uniform(jax.random.fold_in(own, axis_at), (shards_of,), jnp.float32, least / len(shards), high / len(shards)))
        factor_of = factor_of * jnp.repeat(draws, dims[axis_at] // shards_of).reshape([-1 if axis == axis_at else 1 for axis in range(len(dims))])
    return factor_of


def setup_inputs(seed: int = 0) -> dict:
    keys = jax.random.split(jax.random.key(seed), 6)
    src_coords = draw_src_coords(jax.random.fold_in(keys[5], 71), 0)
    tgt_coords = jnp.clip(1.0 * jax.random.uniform(keys[1], (3, NT), jnp.float32) ** steps_of(keys[1], (3, NT), ((1, 16),), -0.2, 0.2), 0.0, 1.0)
    src_scaling = jnp.clip(jnp.exp(math.log(4.0) - 2.7725887 * jax.random.uniform(keys[2], (WEIGHTS, NS), jnp.float32) ** steps_of(keys[2], (WEIGHTS, NS), ((0, 16), (1, 16)), -0.2, 0.2)), 0.25, 4.0)
    src_mass = jnp.clip(jnp.exp(math.log(4.0) - 2.7725887 * jax.random.uniform(keys[3], (WEIGHTS, NS), jnp.float32) ** steps_of(keys[3], (WEIGHTS, NS), ((0, 16), (1, 16)), -0.2, 0.2)), 0.25, 4.0)
    tgt_mass = jnp.clip(jnp.exp(math.log(4.0) - 2.7725887 * jax.random.uniform(keys[4], (WEIGHTS, NT), jnp.float32) ** steps_of(keys[4], (WEIGHTS, NT), ((1, 16),), -0.2, 0.2)), 0.25, 4.0)
    return {"src_coords": src_coords, "tgt_coords": tgt_coords, "src_scaling": src_scaling, "src_mass": src_mass, "tgt_mass": tgt_mass}


def kernel_block(xb, yt):
    dist = (xb[0][:, None] - yt[0][None, :]) ** 2
    dist = dist + (xb[1][:, None] - yt[1][None, :]) ** 2
    dist = dist + (xb[2][:, None] - yt[2][None, :]) ** 2
    return (180.0 * jnp.exp(-100.0 * dist)).astype(jnp.bfloat16)


def reference(src_coords, tgt_coords, src_scaling, src_mass, tgt_mass):
    block = 512
    count = NS // block
    xs_blocks = src_coords.reshape(3, count, block).transpose(1, 0, 2)
    src_low = src_scaling.astype(jnp.bfloat16)
    u_blocks = src_low.reshape(WEIGHTS, count, block).transpose(1, 0, 2)

    def col_step(carry, items):
        xb, ub = items
        kern = kernel_block(xb, tgt_coords)
        return carry + jnp.dot(ub, kern, preferred_element_type=jnp.float32), None

    col_sums, _ = lax.scan(col_step, jnp.zeros((WEIGHTS, NT), jnp.float32), (xs_blocks, u_blocks))
    tgt_scaling = tgt_mass / (col_sums / NS)
    tgt_low = tgt_scaling.astype(jnp.bfloat16)

    def row_step(xb):
        kern = kernel_block(xb, tgt_coords)
        return jnp.dot(tgt_low, kern.T, preferred_element_type=jnp.float32)

    rows = lax.map(row_step, xs_blocks)
    row_sums = rows.transpose(1, 0, 2).reshape(WEIGHTS, NS)
    new_src_scaling = src_mass / (row_sums / NT)
    return new_src_scaling, tgt_scaling
```

```python
import functools
import math

import jax
import jax.numpy as jnp
from jax import lax
from jax.experimental import pallas as pl
from jax.experimental.pallas import tpu as pltpu
from jax.sharding import PartitionSpec as P

F32, BF16 = jnp.float32, jnp.bfloat16
MESH = pl.DeviceIdType.MESH
RATE = 100.0 / math.log(2.0)
TILE = 1024
CHUNKS = 3
DEPTH = 32


def split3(values):
    first = lax.reduce_precision(values, 8, 7)
    rest = values - first
    second = lax.reduce_precision(rest, 8, 7)
    return first, second, lax.reduce_precision(rest - second, 8, 7)


def factors(src_coords, tgt_coords):
    xc, yc = src_coords - 0.5, tgt_coords - 0.5
    xs, ys = split3(2.0 * RATE * xc), split3(yc)
    xa = split3(-RATE * jnp.sum(xc * xc, 0, keepdims=True))
    yb = split3(math.log2(180.0) - RATE * jnp.sum(yc * yc, 0, keepdims=True))
    left, right = [], []
    for p, q in ((0, 0), (0, 1), (1, 0), (1, 1), (0, 2), (2, 0), (1, 2), (2, 1)):
        left.append(xs[p])
        right.append(ys[q])
    for part in range(3):
        left += [xa[part], jnp.ones_like(xa[part])]
        right += [jnp.ones_like(yb[part]), yb[part]]
    left, right = jnp.concatenate(left, 0), jnp.concatenate(right, 0)
    pad = ((0, DEPTH - left.shape[0]), (0, 0))
    return jnp.pad(left, pad).astype(BF16).T, jnp.pad(right, pad).astype(BF16)


def fold(rows):
    n = rows.shape[1]
    return rows.reshape(2, CHUNKS, 8, n // (8 * CHUNKS)).transpose(1, 0, 2, 3).reshape(CHUNKS, 16, n // (8 * CHUNKS))


def unfold(parts):
    wide = parts.shape[2]
    return parts.reshape(CHUNKS, 2, 8, wide).transpose(1, 0, 2, 3).reshape(2, CHUNKS * 8 * wide)


def kernel(
    total, x_ref, y_ref, u_ref, cm_ref, rm_ref,
    new_ref, tgt_ref, far_ref,
    near, stage, u_in, v_in, u_all, v_all, shuffle, col_acc, row_acc, col_out, row_out, col_in, row_in,
    stage_sem, u_send, u_recv, v_send, v_recv, col_send, col_recv, row_send, row_recv,
):
    src, tgt = lax.axis_index("src"), lax.axis_index("tgt")
    peers = lax.axis_size("src")
    blocks = y_ref.shape[1] // TILE
    tiles = x_ref.shape[0] // TILE
    wide = u_ref.shape[2]
    span = 8 * wide
    stored = near.shape[0]
    far = blocks - stored

    def each_peer(body):
        def step(r, carry):
            body(r)
            return carry
        lax.fori_loop(1, peers, step, 0)

    barrier = pltpu.get_barrier_semaphore()

    def greet(r):
        pl.semaphore_signal(barrier, inc=1, device_id={"src": lax.rem(src + r, peers)}, device_id_type=MESH)
        pl.semaphore_signal(barrier, inc=1, device_id={"tgt": lax.rem(tgt + r, peers)}, device_id_type=MESH)

    each_peer(greet)
    u_in[tgt] = u_ref[...]
    pl.semaphore_wait(barrier, 2 * (peers - 1))

    def gather_copy(buf, axis, me, r, send, recv):
        return pltpu.make_async_remote_copy(
            src_ref=buf.at[me], dst_ref=buf.at[me], send_sem=send, recv_sem=recv,
            device_id={axis: lax.rem(me + r, peers)}, device_id_type=MESH,
        )

    def scatter_copy(out, into, axis, me, r, send, recv):
        peer = lax.rem(me + r, peers)
        return pltpu.make_async_remote_copy(
            src_ref=out.at[peer], dst_ref=into.at[r - 1], send_sem=send, recv_sem=recv,
            device_id={axis: peer}, device_id_type=MESH,
        )

    def wait_all(buf, axis, me, send, recv):
        group = buf.at[pl.ds(0, peers - 1)]
        copy = pltpu.make_async_remote_copy(
            src_ref=group, dst_ref=group, send_sem=send, recv_sem=recv,
            device_id={axis: lax.rem(me + 1, peers)}, device_id_type=MESH,
        )
        return copy

    each_peer(lambda r: gather_copy(u_in, "tgt", tgt, r, u_send, u_recv).start())

    def rows_at(i):
        return pl.ds(pl.multiple_of(i * TILE, TILE), TILE)

    def make_tile(b, i):
        e = jnp.dot(x_ref[rows_at(i), :], y_ref[:, b * TILE:(b + 1) * TILE], preferred_element_type=F32)
        return jnp.exp2(e).astype(BF16)

    def ordered(parts, all_ref, at):
        for d in range(peers):
            part = parts(d).astype(F32)
            for h in range(wide // 128):
                shuffle[h, d * 16:(d + 1) * 16, :] = part[:, h * 128:(h + 1) * 128]
        for k in range(8):
            for h in range(wide // 128):
                lanes = at + k * wide + h * 128
                all_ref[:, lanes:lanes + 128] = shuffle[h, pl.ds(k, 2 * peers, stride=8), :].astype(BF16)

    def scattered(acc, at, out):
        for k in range(8):
            for h in range(wide // 128):
                lanes = at + k * wide + h * 128
                shuffle[h, pl.ds(k, 2 * peers, stride=8), :] = acc[:, lanes:lanes + 128]
        for d in range(peers):
            for h in range(wide // 128):
                out[d, :, h * 128:(h + 1) * 128] = shuffle[h, d * 16:(d + 1) * 16, :]

    def summed(out, into, me):
        value = out[me]
        for r in range(peers - 1):
            value = value + into[r]
        return value

    def make_only(b):
        def step(i, carry):
            near[b - far, rows_at(i), :] = make_tile(b, i)
            return carry
        lax.fori_loop(0, tiles, step, 0)

    def use_only(b):
        def step(i, acc):
            return acc + jnp.dot(u_all[:, rows_at(i)], near[b - far, rows_at(i), :], preferred_element_type=F32)
        col_acc[:, b * TILE:(b + 1) * TILE] = lax.fori_loop(0, tiles, step, jnp.zeros((2 * peers, TILE), F32))

    def make_and_use(b):
        def step(i, acc):
            tile = make_tile(b, i)
            if b >= far:
                near[b - far, rows_at(i), :] = tile
            else:
                slot = lax.rem(i, 3)
                if b == 0:
                    @pl.when(i >= 3)
                    def _():
                        pltpu.make_async_copy(stage.at[slot], far_ref.at[b, 0], stage_sem.at[slot]).wait()
                else:
                    pltpu.make_async_copy(stage.at[slot], far_ref.at[b, 0], stage_sem.at[slot]).wait()
                stage[slot] = tile
                pltpu.make_async_copy(stage.at[slot], far_ref.at[b, i], stage_sem.at[slot]).start()
            return acc + jnp.dot(u_all[:, rows_at(i)], tile, preferred_element_type=F32)
        col_acc[:, b * TILE:(b + 1) * TILE] = lax.fori_loop(0, tiles, step, jnp.zeros((2 * peers, TILE), F32))

    def send_cols(c):
        scattered(col_acc, c * span, col_out.at[c])
        each_peer(lambda r: scatter_copy(col_out.at[c], col_in.at[c], "src", src, r, col_send.at[c], col_recv.at[c]).start())

    def turn_cols(c):
        wait_all(col_in.at[c], "src", src, col_send.at[c], col_recv.at[c]).wait_recv()
        value = cm_ref[c] / (summed(col_out.at[c], col_in.at[c], src) / total)
        tgt_ref[c] = value
        v_in[c, src] = value.astype(BF16)
        each_peer(lambda r: gather_copy(v_in.at[c], "src", src, r, v_send.at[c], v_recv.at[c]).start())

    def take_cols(c):
        wait_all(v_in.at[c], "src", src, v_send.at[c], v_recv.at[c]).wait_recv()
        ordered(lambda d: v_in[c, d], v_all, c * span)

    make_only(3)
    make_only(4)
    wait_all(u_in, "tgt", tgt, u_send, u_recv).wait_recv()
    for c in range(CHUNKS):
        ordered(lambda d: u_in[d, c], u_all, c * span)
    make_and_use(0)
    make_and_use(1)
    send_cols(0)
    make_and_use(2)
    use_only(3)
    send_cols(1)
    turn_cols(0)
    use_only(4)
    make_and_use(5)
    send_cols(2)
    turn_cols(1)

    count = far * tiles

    def fetch(t):
        slot = lax.rem(t, 3)
        return pltpu.make_async_copy(far_ref.at[lax.div(t, tiles), lax.rem(t, tiles)], stage.at[slot], stage_sem.at[slot])

    for slot in range(3):
        pltpu.make_async_copy(stage.at[slot], far_ref.at[far - 1, 0], stage_sem.at[slot]).wait()
    for t in range(3):
        fetch(t).start()

    def far_block(b):
        def step(i, carry):
            t = b * tiles + i
            fetch(t).wait()
            part = lax.dot_general(
                v_all[:, b * TILE:(b + 1) * TILE], stage[lax.rem(t, 3)], (((1,), (1,)), ((), ())), preferred_element_type=F32
            )
            if b == 0:
                row_acc[:, rows_at(i)] = part
            else:
                row_acc[:, rows_at(i)] += part

            @pl.when(t + 3 < count)
            def _():
                fetch(t + 3).start()
            return carry
        lax.fori_loop(0, tiles, step, 0)

    take_cols(0)
    far_block(0)
    turn_cols(2)
    far_block(1)
    take_cols(1)
    far_block(2)
    take_cols(2)
    per = span // TILE
    for c in range(CHUNKS):
        def step(i, carry):
            part = row_acc[:, rows_at(i)]
            for b in range(far, blocks):
                part = part + lax.dot_general(
                    v_all[:, b * TILE:(b + 1) * TILE], near[b - far, rows_at(i), :], (((1,), (1,)), ((), ())),
                    preferred_element_type=F32,
                )
            row_acc[:, rows_at(i)] = part
            return carry
        lax.fori_loop(c * per, (c + 1) * per, step, 0)
        scattered(row_acc, c * span, row_out.at[c])
        each_peer(lambda r: scatter_copy(row_out.at[c], row_in.at[c], "tgt", tgt, r, row_send.at[c], row_recv.at[c]).start())
    for c in range(CHUNKS):
        wait_all(row_in.at[c], "tgt", tgt, row_send.at[c], row_recv.at[c]).wait_recv()
        new_ref[c] = rm_ref[c] / (summed(row_out.at[c], row_in.at[c], tgt) / total)
    wait_all(u_in, "tgt", tgt, u_send, u_recv).wait_send()
    for c in range(CHUNKS):
        wait_all(col_in.at[c], "src", src, col_send.at[c], col_recv.at[c]).wait_send()
        wait_all(v_in.at[c], "src", src, v_send.at[c], v_recv.at[c]).wait_send()
        wait_all(row_in.at[c], "tgt", tgt, row_send.at[c], row_recv.at[c]).wait_send()


def on_device(src_coords, tgt_coords, src_scaling, src_mass, tgt_mass):
    pts = src_coords.shape[1]
    peers = lax.axis_size("src")
    total = float(pts * peers)
    x, y = factors(src_coords, tgt_coords)
    mass = lax.dynamic_slice_in_dim(tgt_mass, lax.axis_index("src") * 2, 2, 0)
    wide = pts // (8 * CHUNKS)
    blocks, tiles = pts // TILE, pts // TILE
    stored = blocks // 2
    vmem = pl.BlockSpec(memory_space=pltpu.VMEM)
    dma = pltpu.SemaphoreType.DMA
    new, out, _ = pl.pallas_call(
        functools.partial(kernel, total),
        out_shape=(
            jax.ShapeDtypeStruct((CHUNKS, 16, wide), F32),
            jax.ShapeDtypeStruct((CHUNKS, 16, wide), F32),
            jax.ShapeDtypeStruct((blocks - stored, tiles, TILE, TILE), BF16),
        ),
        in_specs=[vmem] * 5,
        out_specs=(vmem, vmem, pl.BlockSpec(memory_space=pl.ANY)),
        scratch_shapes=[
            pltpu.VMEM((stored, pts, TILE), BF16),
            pltpu.VMEM((3, TILE, TILE), BF16),
            pltpu.VMEM((peers, CHUNKS, 16, wide), BF16),
            pltpu.VMEM((CHUNKS, peers, 16, wide), BF16),
            pltpu.VMEM((2 * peers, pts), BF16),
            pltpu.VMEM((2 * peers, pts), BF16),
            pltpu.VMEM((wide // 128, 16 * peers, 128), F32),
            pltpu.VMEM((2 * peers, pts), F32),
            pltpu.VMEM((2 * peers, pts), F32),
            pltpu.VMEM((CHUNKS, peers, 16, wide), F32),
            pltpu.VMEM((CHUNKS, peers, 16, wide), F32),
            pltpu.VMEM((CHUNKS, peers - 1, 16, wide), F32),
            pltpu.VMEM((CHUNKS, peers - 1, 16, wide), F32),
            dma((3,)), dma, dma, dma((CHUNKS,)), dma((CHUNKS,)),
            dma((CHUNKS,)), dma((CHUNKS,)), dma((CHUNKS,)), dma((CHUNKS,)),
        ],
        compiler_params=pltpu.CompilerParams(
            collective_id=0, has_side_effects=True, vmem_limit_bytes=60 * 2**20
        ),
    )(x, y, fold(src_scaling.astype(BF16)), fold(mass), fold(src_mass))
    return unfold(new), unfold(out)


def solution(mesh):
    placed = (P(None, "src"), P(None, "tgt"), P("tgt", "src"), P("tgt", "src"), P(None, "tgt"))
    return jax.shard_map(
        on_device,
        mesh=mesh,
        in_specs=placed,
        out_specs=(P("tgt", "src"), P("src", "tgt")),
        check_vma=False,
    )
```

```python
import functools
import math

import jax
import jax.numpy as jnp
from jax import lax
from jax.experimental import pallas as pl
from jax.experimental.pallas import tpu as pltpu
from jax.sharding import PartitionSpec as P

F32, BF16 = jnp.float32, jnp.bfloat16
MESH = pl.DeviceIdType.MESH
RATE = 100.0 / math.log(2.0)
TILE = 1024
CHUNKS = 3
DEPTH = 128
LANES = 128


def split3(values):
    first = values.astype(BF16).astype(F32)
    rest = values - first
    second = rest.astype(BF16).astype(F32)
    return first, second, rest - second


def kernel(
    total, xc_ref, yc_ref, sc_ref, rm_ref, cm_ref,
    new_ref, tgt_ref, far_ref,
    near, stage, x_fac, y_fac, u_in, v_in, u_all, v_all, shuffle, col_acc, row_acc, col_mass, row_mass,
    col_out, col_in, row_out, row_x, row_half, row_in,
    stage_sem, u_send, u_recv, v_send, v_recv, col_send, col_recv, x_send, x_recv, row_send, row_recv,
):
    src, tgt = lax.axis_index("src"), lax.axis_index("tgt")
    peers = lax.axis_size("src")
    weights = 2 * peers
    pts = sc_ref.shape[1]
    blocks = tiles = pts // TILE
    stored = near.shape[0]
    span = pts // CHUNKS
    half = peers // 2
    xh, z = lax.div(tgt, half), lax.rem(tgt, half)

    def each_peer(body, count=peers):
        def step(r, carry):
            body(r)
            return carry
        lax.fori_loop(1, count, step, 0)

    barrier = pltpu.get_barrier_semaphore()

    def greet(r):
        pl.semaphore_signal(barrier, inc=1, device_id={"src": lax.rem(src + r, peers)}, device_id_type=MESH)
        pl.semaphore_signal(barrier, inc=1, device_id={"tgt": lax.rem(tgt + r, peers)}, device_id_type=MESH)

    each_peer(greet)

    def folded(out, rows_of, at, cols):
        wide = cols // LANES
        for w in range(2):
            for k in range(wide):
                out[w * wide + k:w * wide + k + 1, :] = rows_of(w, at + k * LANES)

    def unfolded(ref, at, value):
        wide = value.shape[0] // 2
        for w in range(2):
            for k in range(wide):
                ref[w:w + 1, pl.ds(at + k * LANES, LANES)] = value[w * wide + k:w * wide + k + 1, :]

    def ordered(parts, all_ref, at, cols):
        wide = cols // LANES
        for d in range(peers):
            shuffle[d * 2 * wide:(d + 1) * 2 * wide, :] = parts[d].astype(F32)
        for k in range(wide):
            lanes = at + k * LANES
            all_ref[:, lanes:lanes + LANES] = shuffle[pl.ds(k, weights, stride=wide), :].astype(BF16)

    def scattered(acc, at, cols, out):
        wide = cols // LANES
        for k in range(wide):
            out[pl.ds(k, weights, stride=wide), :] = acc[:, pl.ds(at + k * LANES, LANES)]

    folded(shuffle, lambda w, lane: sc_ref[w:w + 1, lane:lane + LANES], 0, pts)
    u_in[tgt] = shuffle[:u_in.shape[1], :].astype(BF16)
    group = cm_ref[pl.ds(pl.multiple_of(lax.div(src, 4) * 8, 8), 8), :]
    place = lax.rem(src, 4)
    own = jnp.where(place < 2, jnp.where(place == 0, group[0:2], group[2:4]), jnp.where(place == 2, group[4:6], group[6:8]))
    for c in range(CHUNKS):
        folded(col_mass.at[c], lambda w, lane: own[w:w + 1, lane:lane + LANES], c * span, span)
    for c in range(tiles):
        folded(row_mass.at[c], lambda w, lane: rm_ref[w:w + 1, lane:lane + LANES], c * TILE, TILE)

    pl.semaphore_wait(barrier, 2 * (peers - 1))

    def gather_copy(buf, axis, me, r, send, recv):
        return pltpu.make_async_remote_copy(
            src_ref=buf.at[me], dst_ref=buf.at[me], send_sem=send, recv_sem=recv,
            device_id={axis: lax.rem(me + r, peers)}, device_id_type=MESH,
        )

    def group_copy(group, axis, peer, send, recv):
        return pltpu.make_async_remote_copy(
            src_ref=group, dst_ref=group, send_sem=send, recv_sem=recv,
            device_id={axis: peer}, device_id_type=MESH,
        )

    def u_group():
        return group_copy(u_in.at[pl.ds(0, peers - 1)], "tgt", lax.rem(tgt + 1, peers), u_send, u_recv)

    def v_group(c):
        return group_copy(v_in.at[c, pl.ds(0, peers - 1)], "src", lax.rem(src + 1, peers), v_send.at[c], v_recv.at[c])

    def col_group(c):
        return group_copy(col_in.at[c], "src", lax.rem(src + 1, peers), col_send.at[c], col_recv.at[c])

    def row_group(c):
        return group_copy(row_in.at[c], "tgt", xh * half + lax.rem(z + 1, half), row_send.at[c], row_recv.at[c])

    each_peer(lambda r: gather_copy(u_in, "tgt", tgt, r, u_send, u_recv).start())

    def factor_rows(out, parts, own_at, ones_at, own):
        for n, part in enumerate(parts):
            out[3 * n:3 * n + 3, :] = part
        for n, part in enumerate(own):
            out[own_at + n:own_at + n + 1, :] = part
            out[ones_at + n:ones_at + n + 1, :] = jnp.ones_like(part)
        out[30:32, :] = jnp.zeros((2, pts), F32)

    def squares(values):
        return values[0:1] * values[0:1] + values[1:2] * values[1:2] + values[2:3] * values[2:3]

    xc, yc = xc_ref[...] - 0.5, yc_ref[...] - 0.5
    xs, ys = split3((2.0 * RATE) * xc), split3(yc)
    pairs = ((0, 0), (0, 1), (1, 0), (1, 1), (0, 2), (2, 0), (1, 2), (2, 1))
    factor_rows(col_acc, [xs[p] for p, _ in pairs], 24, 27, split3(-RATE * squares(xc)))
    factor_rows(row_acc, [ys[q] for _, q in pairs], 27, 24, split3(math.log2(180.0) - RATE * squares(yc)))

    def rows_at(i):
        return pl.ds(pl.multiple_of(i * TILE, TILE), TILE)

    def lay(i, carry):
        zeros = jnp.zeros((DEPTH - 32, TILE), F32)
        x_fac[rows_at(i), :] = jnp.concatenate([col_acc[0:32, rows_at(i)], zeros], 0).T.astype(BF16)
        y_fac[0:32, rows_at(i)] = row_acc[0:32, rows_at(i)].astype(BF16)
        y_fac[32:, rows_at(i)] = zeros.astype(BF16)
        return carry

    lax.fori_loop(0, tiles, lay, 0)

    def make_tile(b, i):
        e = jnp.dot(x_fac[rows_at(i), :], y_fac[:, rows_at(b)], preferred_element_type=F32)
        return jnp.exp2(e).astype(BF16)

    def make_only(t, carry):
        b, i = lax.div(t, tiles), lax.rem(t, tiles)
        near[b, rows_at(i), :] = make_tile(b, i)
        return carry

    def use_only(b):
        def step(i, acc):
            return acc + jnp.dot(u_all[:, rows_at(i)], near[b, rows_at(i), :], preferred_element_type=F32)
        col_acc[:, b * TILE:(b + 1) * TILE] = lax.fori_loop(0, tiles, step, jnp.zeros((weights, TILE), F32))

    def stored_copy(slot, f, i):
        return pltpu.make_async_copy(stage.at[slot], far_ref.at[f, i], stage_sem.at[slot])

    def make_and_use(b):
        f = b - stored

        def step(i, acc):
            slot = lax.rem(i, 3)
            tile = make_tile(b, i)
            if f == 0:
                @pl.when(i >= 3)
                def _():
                    stored_copy(slot, f, 0).wait()
            else:
                stored_copy(slot, f, 0).wait()
            stage[slot] = tile
            stored_copy(slot, f, i).start()
            return acc + jnp.dot(u_all[:, rows_at(i)], tile, preferred_element_type=F32)
        col_acc[:, b * TILE:(b + 1) * TILE] = lax.fori_loop(0, tiles, step, jnp.zeros((weights, TILE), F32))

    def send_cols(c):
        scattered(col_acc, c * span, span, col_out.at[c])
        rows = 2 * span // LANES

        def send(r):
            peer = lax.rem(src + r, peers)
            pltpu.make_async_remote_copy(
                src_ref=col_out.at[c, pl.ds(pl.multiple_of(peer * rows, rows), rows)], dst_ref=col_in.at[c, r - 1],
                send_sem=col_send.at[c], recv_sem=col_recv.at[c],
                device_id={"src": peer}, device_id_type=MESH,
            ).start()
        each_peer(send)

    def turn_cols(c):
        rows = 2 * span // LANES
        col_group(c).wait_recv()
        value = col_out[c, pl.ds(pl.multiple_of(src * rows, rows), rows)]
        for r in range(peers - 1):
            value = value + col_in[c, r]
        value = col_mass[c] / (value / total)
        v_in[c, src] = value.astype(BF16)
        each_peer(lambda r: gather_copy(v_in.at[c], "src", src, r, v_send.at[c], v_recv.at[c]).start())
        unfolded(tgt_ref, c * span, value)

    def take_cols(c):
        v_group(c).wait_recv()
        ordered(v_in.at[c], v_all, c * span, span)

    lax.fori_loop(0, stored * tiles, make_only, 0)
    u_group().wait_recv()
    ordered(u_in, u_all, 0, pts)
    use_only(0)
    use_only(1)
    send_cols(0)
    use_only(2)
    make_and_use(3)
    send_cols(1)
    turn_cols(0)
    make_and_use(4)
    turn_cols(1)
    make_and_use(5)
    send_cols(2)

    count = (blocks - stored) * tiles

    def fetch(t):
        early = t < tiles
        f = jnp.where(early, 0, 1 + lax.rem(t, 2))
        i = jnp.where(early, t, lax.div(t - tiles, 2))
        slot = lax.rem(t, 3)
        return pltpu.make_async_copy(far_ref.at[f, i], stage.at[slot], stage_sem.at[slot])

    def fetch_later(t):
        @pl.when(t < count)
        def _():
            fetch(t).start()

    for slot in range(3):
        stored_copy(slot, 0, 0).wait()
    for t in range(3):
        fetch(t).start()

    def by_rows(b, tile):
        return lax.dot_general(
            v_all[:, b * TILE:(b + 1) * TILE], tile, (((1,), (1,)), ((), ())), preferred_element_type=F32
        )

    def near_block(b):
        def step(i, carry):
            part = by_rows(b, near[b, rows_at(i), :])
            if b == 0:
                row_acc[:, rows_at(i)] = part
            else:
                row_acc[:, rows_at(i)] += part
            return carry
        lax.fori_loop(0, tiles, step, 0)

    def far_step(t, carry):
        fetch(t).wait()
        row_acc[:, rows_at(t)] += by_rows(stored, stage[lax.rem(t, 3)])
        fetch_later(t + 3)
        return carry

    own_rows = 2 * TILE // LANES
    half_rows = half * own_rows

    def cross(c):
        return pltpu.make_async_remote_copy(
            src_ref=row_out.at[c, pl.ds(pl.multiple_of((1 - xh) * half_rows, half_rows), half_rows)], dst_ref=row_x.at[c],
            send_sem=x_send.at[c], recv_sem=x_recv.at[c],
            device_id={"tgt": lax.rem(tgt + half, peers)}, device_id_type=MESH,
        )

    def along(c):
        cross(c).wait_recv()
        row_half[c] = row_out[c, pl.ds(pl.multiple_of(xh * half_rows, half_rows), half_rows)] + row_x[c]

        def send(r):
            to = lax.rem(z + r, half)
            pltpu.make_async_remote_copy(
                src_ref=row_half.at[c, pl.ds(pl.multiple_of(to * own_rows, own_rows), own_rows)], dst_ref=row_in.at[c, r - 1],
                send_sem=row_send.at[c], recv_sem=row_recv.at[c],
                device_id={"tgt": xh * half + to}, device_id_type=MESH,
            ).start()
        each_peer(send, half)

    def last_step(c, carry):
        part = row_acc[:, rows_at(c)] + by_rows(2, near[2, rows_at(c), :])
        for n in range(2):
            t = tiles + 2 * c + n
            fetch(t).wait()
            part = part + by_rows(stored + 1 + n, stage[lax.rem(t, 3)])
            fetch_later(t + 3)
        row_acc[:, rows_at(c)] = part
        scattered(row_acc, c * TILE, TILE, row_out.at[c])
        cross(c).start()

        @pl.when(c > 0)
        def _():
            along(c - 1)
        return carry

    take_cols(0)
    near_block(0)
    near_block(1)
    turn_cols(2)
    take_cols(1)
    lax.fori_loop(0, tiles, far_step, 0)
    take_cols(2)
    lax.fori_loop(0, tiles, last_step, 0)
    along(tiles - 1)

    def finish(c, carry):
        row_group(c).wait_recv()
        value = row_half[c, pl.ds(pl.multiple_of(z * own_rows, own_rows), own_rows)]
        for r in range(half - 1):
            value = value + row_in[c, r]
        unfolded(new_ref, pl.multiple_of(c * TILE, TILE), row_mass[c] / (value / total))
        row_group(c).wait_send()
        cross(c).wait_send()
        return carry

    lax.fori_loop(0, tiles, finish, 0)
    u_group().wait_send()
    for c in range(CHUNKS):
        col_group(c).wait_send()
        v_group(c).wait_send()


def on_device(src_coords, tgt_coords, src_scaling, src_mass, tgt_mass):
    pts = src_coords.shape[1]
    weights = tgt_mass.shape[0]
    peers = lax.axis_size("src")
    total = float(pts * peers)
    tiles = pts // TILE
    stored = tiles // 2
    span = pts // CHUNKS
    half = peers // 2
    piece, tile_piece = 2 * span // LANES, 2 * TILE // LANES
    vmem = pl.BlockSpec(memory_space=pltpu.VMEM)
    dma = pltpu.SemaphoreType.DMA
    scratch = [
        ((stored, pts, TILE), BF16),
        ((3, TILE, TILE), BF16),
        ((pts, DEPTH), BF16),
        ((DEPTH, pts), BF16),
        ((peers, 2 * pts // LANES, LANES), BF16),
        ((CHUNKS, peers, piece, LANES), BF16),
        ((weights, pts), BF16),
        ((weights, pts), BF16),
        ((weights * pts // LANES, LANES), F32),
        ((weights, pts), F32),
        ((weights, pts), F32),
        ((CHUNKS, piece, LANES), F32),
        ((tiles, tile_piece, LANES), F32),
        ((CHUNKS, peers * piece, LANES), F32),
        ((CHUNKS, peers - 1, piece, LANES), F32),
        ((tiles, peers * tile_piece, LANES), F32),
        ((tiles, half * tile_piece, LANES), F32),
        ((tiles, half * tile_piece, LANES), F32),
        ((tiles, half - 1, tile_piece, LANES), F32),
    ]
    new, out, _ = pl.pallas_call(
        functools.partial(kernel, total),
        out_shape=(
            jax.ShapeDtypeStruct((2, pts), F32),
            jax.ShapeDtypeStruct((2, pts), F32),
            jax.ShapeDtypeStruct((tiles - stored, tiles, TILE, TILE), BF16),
        ),
        in_specs=[vmem] * 5,
        out_specs=(vmem, vmem, pl.BlockSpec(memory_space=pl.ANY)),
        scratch_shapes=[pltpu.VMEM(shape, dtype) for shape, dtype in scratch] + [
            dma((3,)), dma, dma, dma((CHUNKS,)), dma((CHUNKS,)), dma((CHUNKS,)), dma((CHUNKS,)),
            dma((tiles,)), dma((tiles,)), dma((tiles,)), dma((tiles,)),
        ],
        compiler_params=pltpu.CompilerParams(
            collective_id=0, has_side_effects=True, vmem_limit_bytes=60 * 2**20
        ),
    )(src_coords, tgt_coords, src_scaling, src_mass, tgt_mass)
    return new, out


def solution(mesh):
    placed = (P(None, "src"), P(None, "tgt"), P("tgt", "src"), P("tgt", "src"), P(None, "tgt"))
    return jax.shard_map(
        on_device,
        mesh=mesh,
        in_specs=placed,
        out_specs=(P("tgt", "src"), P("src", "tgt")),
        check_vma=False,
    )
```

```python
import functools
import math

import jax
import jax.numpy as jnp
from jax import lax
from jax.experimental import pallas as pl
from jax.experimental.pallas import tpu as pltpu
from jax.sharding import PartitionSpec as P

F32, BF16 = jnp.float32, jnp.bfloat16
MESH = pl.DeviceIdType.MESH
RATE = 100.0 / math.log(2.0)
TILE = 1024
PIECE = 256
CHUNKS = 3
DEPTH = 128
LANES = 128


def split3(values):
    first = values.astype(BF16).astype(F32)
    rest = values - first
    second = rest.astype(BF16).astype(F32)
    return first, second, rest - second


def kernel(
    total, xc_ref, yc_ref, sc_ref, rm_ref, cm_ref,
    new_ref, tgt_ref, far_ref,
    near0, near1, near2, stage0, stage1, stage2, x_fac, y_fac, u_in, v_in, u_all, v_all, shuffle, col_acc, row_acc, col_mass, row_mass,
    col_out, col_in, row_out, row_x, row_half, row_in,
    stage_sem, u_send, u_recv, v_send, v_recv, col_send, col_recv, x_send, x_recv, row_send, row_recv,
):
    src, tgt = lax.axis_index("src"), lax.axis_index("tgt")
    peers = lax.axis_size("src")
    weights = 2 * peers
    pts = sc_ref.shape[1]
    blocks = tiles = pts // TILE
    near, stage = (near0, near1, near2), (stage0, stage1, stage2)
    slots, far = len(stage), blocks - len(near)
    span = pts // CHUNKS
    half = peers // 2
    xh, z = lax.div(tgt, half), lax.rem(tgt, half)

    def each_peer(body, count=peers):
        def step(r, carry):
            body(r)
            return carry
        lax.fori_loop(1, count, step, 0)

    barrier = pltpu.get_barrier_semaphore()

    def greet(r):
        pl.semaphore_signal(barrier, inc=1, device_id={"src": lax.rem(src + r, peers)}, device_id_type=MESH)
        pl.semaphore_signal(barrier, inc=1, device_id={"tgt": lax.rem(tgt + r, peers)}, device_id_type=MESH)

    each_peer(greet)

    def folded(out, rows_of, at, cols):
        wide = cols // LANES
        for w in range(2):
            for k in range(wide):
                out[w * wide + k:w * wide + k + 1, :] = rows_of(w, at + k * LANES)

    def unfolded(ref, at, value):
        wide = value.shape[0] // 2
        for w in range(2):
            for k in range(wide):
                ref[w:w + 1, pl.ds(at + k * LANES, LANES)] = value[w * wide + k:w * wide + k + 1, :]

    def ordered(parts, all_ref, at, cols):
        wide = cols // LANES
        for d in range(peers):
            shuffle[d * 2 * wide:(d + 1) * 2 * wide, :] = parts[d].astype(F32)
        for k in range(wide):
            lanes = at + k * LANES
            all_ref[:, lanes:lanes + LANES] = shuffle[pl.ds(k, weights, stride=wide), :].astype(BF16)

    def scattered(acc, at, cols, out):
        wide = cols // LANES
        for k in range(wide):
            out[pl.ds(k, weights, stride=wide), :] = acc[:, pl.ds(at + k * LANES, LANES)]

    folded(shuffle, lambda w, lane: sc_ref[w:w + 1, lane:lane + LANES], 0, pts)
    u_in[tgt] = shuffle[:u_in.shape[1], :].astype(BF16)
    group = cm_ref[pl.ds(pl.multiple_of(lax.div(src, 4) * 8, 8), 8), :]
    place = lax.rem(src, 4)
    own = jnp.where(place < 2, jnp.where(place == 0, group[0:2], group[2:4]), jnp.where(place == 2, group[4:6], group[6:8]))
    for c in range(CHUNKS):
        folded(col_mass.at[c], lambda w, lane: own[w:w + 1, lane:lane + LANES], c * span, span)
    for c in range(tiles):
        folded(row_mass.at[c], lambda w, lane: rm_ref[w:w + 1, lane:lane + LANES], c * TILE, TILE)

    pl.semaphore_wait(barrier, 2 * (peers - 1))

    def gather_copy(buf, axis, me, r, send, recv):
        return pltpu.make_async_remote_copy(
            src_ref=buf.at[me], dst_ref=buf.at[me], send_sem=send, recv_sem=recv,
            device_id={axis: lax.rem(me + r, peers)}, device_id_type=MESH,
        )

    def group_copy(group, axis, peer, send, recv):
        return pltpu.make_async_remote_copy(
            src_ref=group, dst_ref=group, send_sem=send, recv_sem=recv,
            device_id={axis: peer}, device_id_type=MESH,
        )

    def u_group():
        return group_copy(u_in.at[pl.ds(0, peers - 1)], "tgt", lax.rem(tgt + 1, peers), u_send, u_recv)

    def v_group(c):
        return group_copy(v_in.at[c, pl.ds(0, peers - 1)], "src", lax.rem(src + 1, peers), v_send.at[c], v_recv.at[c])

    def col_group(c):
        return group_copy(col_in.at[c], "src", lax.rem(src + 1, peers), col_send.at[c], col_recv.at[c])

    def row_group(c):
        return group_copy(row_in.at[c], "tgt", xh * half + lax.rem(z + 1, half), row_send.at[c], row_recv.at[c])

    each_peer(lambda r: gather_copy(u_in, "tgt", tgt, r, u_send, u_recv).start())

    def factor_rows(out, parts, own_at, ones_at, own):
        for n, part in enumerate(parts):
            out[3 * n:3 * n + 3, :] = part
        for n, part in enumerate(own):
            out[own_at + n:own_at + n + 1, :] = part
            out[ones_at + n:ones_at + n + 1, :] = jnp.ones_like(part)
        out[30:32, :] = jnp.zeros((2, pts), F32)

    def squares(values):
        return values[0:1] * values[0:1] + values[1:2] * values[1:2] + values[2:3] * values[2:3]

    xc, yc = xc_ref[...] - 0.5, yc_ref[...] - 0.5
    xs, ys = split3((2.0 * RATE) * xc), split3(yc)
    pairs = ((0, 0), (0, 1), (1, 0), (1, 1), (0, 2), (2, 0), (1, 2), (2, 1))
    factor_rows(col_acc, [xs[p] for p, _ in pairs], 24, 27, split3(-RATE * squares(xc)))
    factor_rows(row_acc, [ys[q] for _, q in pairs], 27, 24, split3(math.log2(180.0) - RATE * squares(yc)))

    def rows_at(i):
        return pl.ds(pl.multiple_of(i * TILE, TILE), TILE)

    def lay(i, carry):
        zeros = jnp.zeros((DEPTH - 32, TILE), F32)
        x_fac[rows_at(i), :] = jnp.concatenate([col_acc[0:32, rows_at(i)], zeros], 0).T.astype(BF16)
        y_fac[0:32, rows_at(i)] = row_acc[0:32, rows_at(i)].astype(BF16)
        y_fac[32:, rows_at(i)] = zeros.astype(BF16)
        return carry

    lax.fori_loop(0, tiles, lay, 0)

    def make_piece(start, b, i):
        rows = pl.ds(pl.multiple_of(i * TILE + start, PIECE), PIECE)
        e = jnp.dot(x_fac[rows, :], y_fac[:, rows_at(b)], preferred_element_type=F32)
        return jnp.exp2(e).astype(BF16)

    def make_only(b):
        def step(i, carry):
            e = jnp.dot(x_fac[rows_at(i), :], y_fac[:, b * TILE:(b + 1) * TILE], preferred_element_type=F32)
            near[b - far][rows_at(i), :] = jnp.exp2(e).astype(BF16)
            return carry
        lax.fori_loop(0, tiles, step, 0)

    def use_only(b):
        def step(i, acc):
            return acc + jnp.dot(u_all[:, rows_at(i)], near[b - far][rows_at(i), :], preferred_element_type=F32)
        col_acc[:, b * TILE:(b + 1) * TILE] = lax.fori_loop(0, tiles, step, jnp.zeros((weights, TILE), F32))

    def make_and_use(made, used):
        def step(i, acc):
            for start in range(0, TILE, PIECE):
                rows = pl.ds(pl.multiple_of(i * TILE + start, PIECE), PIECE)
                near[made - far][rows, :] = make_piece(start, made, i)
                acc = acc + jnp.dot(u_all[:, rows], near[used - far][rows, :], preferred_element_type=F32)
            return acc
        col_acc[:, used * TILE:(used + 1) * TILE] = lax.fori_loop(0, tiles, step, jnp.zeros((weights, TILE), F32))

    def stored_copy(slot, t):
        return pltpu.make_async_copy(stage[slot], far_ref.at[lax.div(t, tiles), lax.rem(t, tiles)], stage_sem.at[slot])

    def far_steps(first, last):
        def step(n, carry):
            for slot in range(slots):
                t = n * slots + slot
                b, i = lax.div(t, tiles), lax.rem(t, tiles)
                other = (slot + 1) % slots
                later = jnp.minimum(t + 1, far * tiles - 1)
                lb, li = lax.div(later, tiles), lax.rem(later, tiles)

                @pl.when(t + 1 >= slots)
                def _():
                    stored_copy(other, 0).wait()

                stored_copy(slot, t).start()
                acc = jnp.zeros((weights, TILE), F32)
                for start in range(0, TILE, PIECE):
                    piece = slice(start, start + PIECE)
                    stage[other][piece, :] = make_piece(start, lb, li)
                    rows = pl.ds(pl.multiple_of(i * TILE + start, PIECE), PIECE)
                    acc = acc + jnp.dot(u_all[:, rows], stage[slot][piece, :], preferred_element_type=F32)
                col_acc[:, rows_at(b)] += acc
            return carry
        lax.fori_loop(first // slots, last // slots, step, 0)

    def send_cols(c):
        scattered(col_acc, c * span, span, col_out.at[c])
        rows = 2 * span // LANES

        def send(r):
            peer = lax.rem(src + r, peers)
            pltpu.make_async_remote_copy(
                src_ref=col_out.at[c, pl.ds(pl.multiple_of(peer * rows, rows), rows)], dst_ref=col_in.at[c, r - 1],
                send_sem=col_send.at[c], recv_sem=col_recv.at[c],
                device_id={"src": peer}, device_id_type=MESH,
            ).start()
        each_peer(send)

    def turn_cols(c):
        rows = 2 * span // LANES
        col_group(c).wait_recv()
        value = col_out[c, pl.ds(pl.multiple_of(src * rows, rows), rows)]
        for r in range(peers - 1):
            value = value + col_in[c, r]
        value = col_mass[c] / (value / total)
        v_in[c, src] = value.astype(BF16)
        each_peer(lambda r: gather_copy(v_in.at[c], "src", src, r, v_send.at[c], v_recv.at[c]).start())
        unfolded(tgt_ref, c * span, value)

    def take_cols(c):
        v_group(c).wait_recv()
        ordered(v_in.at[c], v_all, c * span, span)

    make_only(3)
    make_only(4)
    for start in range(0, TILE, PIECE):
        stage[0][start:start + PIECE, :] = make_piece(start, 0, 0)
    u_group().wait_recv()
    ordered(u_in, u_all, 0, pts)
    col_acc[:, :far * TILE] = jnp.zeros((weights, far * TILE), F32)
    far_steps(0, 2 * tiles)
    send_cols(0)
    far_steps(2 * tiles, 3 * tiles)
    make_and_use(5, 3)
    send_cols(1)
    turn_cols(0)
    use_only(4)
    use_only(5)
    send_cols(2)

    count = far * tiles

    def fetch(slot, t):
        return pltpu.make_async_copy(far_ref.at[lax.div(t, tiles), lax.rem(t, tiles)], stage[slot], stage_sem.at[slot])

    def fetch_later(slot, t):
        @pl.when(t < count)
        def _():
            fetch(slot, t).start()

    for slot in range(1, slots):
        stored_copy(slot, 0).wait()
    for t in range(slots):
        fetch(t, t).start()

    def by_rows(b, tile):
        return lax.dot_general(
            v_all[:, b], tile, (((1,), (1,)), ((), ())), preferred_element_type=F32
        )

    def far_rows(first, last, fresh):
        def step(n, carry):
            for slot in range(slots):
                t = n * slots + slot
                i = lax.rem(t, tiles)
                fetch(slot, t).wait()
                part = by_rows(rows_at(lax.div(t, tiles)), stage[slot][...])
                if fresh:
                    row_acc[:, rows_at(i)] = part
                else:
                    row_acc[:, rows_at(i)] += part
                fetch_later(slot, t + slots)
            return carry
        lax.fori_loop(first // slots, last // slots, step, 0)

    def near_rows(b):
        def step(i, carry):
            row_acc[:, rows_at(i)] += by_rows(slice(b * TILE, (b + 1) * TILE), near[b - far][rows_at(i), :])
            return carry
        lax.fori_loop(0, tiles, step, 0)

    own_rows = 2 * TILE // LANES
    half_rows = half * own_rows

    def cross(c):
        return pltpu.make_async_remote_copy(
            src_ref=row_out.at[c, pl.ds(pl.multiple_of((1 - xh) * half_rows, half_rows), half_rows)], dst_ref=row_x.at[c],
            send_sem=x_send.at[c], recv_sem=x_recv.at[c],
            device_id={"tgt": lax.rem(tgt + half, peers)}, device_id_type=MESH,
        )

    def along(c):
        cross(c).wait_recv()
        row_half[c] = row_out[c, pl.ds(pl.multiple_of(xh * half_rows, half_rows), half_rows)] + row_x[c]

        def send(r):
            to = lax.rem(z + r, half)
            pltpu.make_async_remote_copy(
                src_ref=row_half.at[c, pl.ds(pl.multiple_of(to * own_rows, own_rows), own_rows)], dst_ref=row_in.at[c, r - 1],
                send_sem=row_send.at[c], recv_sem=row_recv.at[c],
                device_id={"tgt": xh * half + to}, device_id_type=MESH,
            ).start()
        each_peer(send, half)

    def last_steps(n, carry):
        for slot in range(slots):
            c = n * slots + slot
            part = row_acc[:, rows_at(c)]
            for b in (4, 5):
                part = part + by_rows(slice(b * TILE, (b + 1) * TILE), near[b - far][rows_at(c), :])
            t = 2 * tiles + c
            fetch(slot, t).wait()
            part = part + by_rows(slice(2 * TILE, 3 * TILE), stage[slot][...])
            fetch_later(slot, t + slots)
            row_acc[:, rows_at(c)] = part
            scattered(row_acc, pl.multiple_of(c * TILE, TILE), TILE, row_out.at[c])
            cross(c).start()

            @pl.when(c > 0)
            def _():
                along(c - 1)
        return carry

    take_cols(0)
    far_rows(0, tiles, True)
    turn_cols(1)
    far_rows(tiles, tiles + slots, False)
    turn_cols(2)
    far_rows(tiles + slots, 2 * tiles, False)
    take_cols(1)
    near_rows(3)
    take_cols(2)
    lax.fori_loop(0, tiles // slots, last_steps, 0)
    along(tiles - 1)

    def finish(c, carry):
        row_group(c).wait_recv()
        value = row_half[c, pl.ds(pl.multiple_of(z * own_rows, own_rows), own_rows)]
        for r in range(half - 1):
            value = value + row_in[c, r]
        unfolded(new_ref, pl.multiple_of(c * TILE, TILE), row_mass[c] / (value / total))
        row_group(c).wait_send()
        cross(c).wait_send()
        return carry

    lax.fori_loop(0, tiles, finish, 0)
    u_group().wait_send()
    for c in range(CHUNKS):
        col_group(c).wait_send()
        v_group(c).wait_send()


def on_device(src_coords, tgt_coords, src_scaling, src_mass, tgt_mass):
    pts = src_coords.shape[1]
    weights = tgt_mass.shape[0]
    peers = lax.axis_size("src")
    total = float(pts * peers)
    tiles = pts // TILE
    stored = tiles // 2
    span = pts // CHUNKS
    half = peers // 2
    piece, tile_piece = 2 * span // LANES, 2 * TILE // LANES
    vmem = pl.BlockSpec(memory_space=pltpu.VMEM)
    dma = pltpu.SemaphoreType.DMA
    scratch = [
        *[((pts, TILE), BF16)] * stored,
        *[((TILE, TILE), BF16)] * 3,
        ((pts, DEPTH), BF16),
        ((DEPTH, pts), BF16),
        ((peers, 2 * pts // LANES, LANES), BF16),
        ((CHUNKS, peers, piece, LANES), BF16),
        ((weights, pts), BF16),
        ((weights, pts), BF16),
        ((weights * pts // LANES, LANES), F32),
        ((weights, pts), F32),
        ((weights, pts), F32),
        ((CHUNKS, piece, LANES), F32),
        ((tiles, tile_piece, LANES), F32),
        ((CHUNKS, peers * piece, LANES), F32),
        ((CHUNKS, peers - 1, piece, LANES), F32),
        ((tiles, peers * tile_piece, LANES), F32),
        ((tiles, half * tile_piece, LANES), F32),
        ((tiles, half * tile_piece, LANES), F32),
        ((tiles, half - 1, tile_piece, LANES), F32),
    ]
    new, out, _ = pl.pallas_call(
        functools.partial(kernel, total),
        out_shape=(
            jax.ShapeDtypeStruct((2, pts), F32),
            jax.ShapeDtypeStruct((2, pts), F32),
            jax.ShapeDtypeStruct((tiles - stored, tiles, TILE, TILE), BF16),
        ),
        in_specs=[vmem] * 5,
        out_specs=(vmem, vmem, pl.BlockSpec(memory_space=pl.ANY)),
        scratch_shapes=[pltpu.VMEM(shape, dtype) for shape, dtype in scratch] + [
            dma((3,)), dma, dma, dma((CHUNKS,)), dma((CHUNKS,)), dma((CHUNKS,)), dma((CHUNKS,)),
            dma((tiles,)), dma((tiles,)), dma((tiles,)), dma((tiles,)),
        ],
        compiler_params=pltpu.CompilerParams(
            collective_id=0, has_side_effects=True, vmem_limit_bytes=60 * 2**20
        ),
    )(src_coords, tgt_coords, src_scaling, src_mass, tgt_mass)
    return new, out


def solution(mesh):
    placed = (P(None, "src"), P(None, "tgt"), P("tgt", "src"), P("tgt", "src"), P(None, "tgt"))
    return jax.shard_map(
        on_device,
        mesh=mesh,
        in_specs=placed,
        out_specs=(P("tgt", "src"), P("src", "tgt")),
        check_vma=False,
    )
```

```python
import functools
import math

import jax
import jax.numpy as jnp
from jax import lax
from jax.experimental import pallas as pl
from jax.experimental.pallas import tpu as pltpu
from jax.sharding import PartitionSpec as P

F32, BF16 = jnp.float32, jnp.bfloat16
MESH = pl.DeviceIdType.MESH
RATE = 100.0 / math.log(2.0)
TILE = 1024
PIECE = 256
CHUNKS = 3
DEPTH = 128
LANES = 128


def split3(values):
    first = values.astype(BF16).astype(F32)
    rest = values - first
    second = rest.astype(BF16).astype(F32)
    return first, second, rest - second


def kernel(
    total, xc_ref, yc_ref, sc_ref, rm_ref, cm_ref,
    out_ref, far_ref,
    near0, near1, near2, stage0, stage1, stage2, x_fac, y_fac, u_in, v_in, u_all, v_all, shuffle, col_acc, row_acc, col_mass, row_mass,
    col_out, col_in, row_out, row_x, row_half, row_in, last_in,
    stage_sem, u_send, u_recv, v_send, v_recv, col_send, col_recv, x_send, x_recv, row_send, row_recv, last_send, last_recv,
):
    src, tgt = lax.axis_index("src"), lax.axis_index("tgt")
    peers = lax.axis_size("src")
    weights = 2 * peers
    pts = sc_ref.shape[1]
    blocks = tiles = pts // TILE
    new_ref, tgt_ref = out_ref.at[0], out_ref.at[1]
    near, stage = (near0, near1, near2), (stage0, stage1, stage2)
    slots, far = len(stage), blocks - len(near)
    span = pts // CHUNKS
    half = peers // 2
    xh, z = lax.div(tgt, half), lax.rem(tgt, half)

    def each_peer(body, count=peers):
        def step(r, carry):
            body(r)
            return carry
        lax.fori_loop(1, count, step, 0)

    barrier = pltpu.get_barrier_semaphore()

    def greet(r):
        pl.semaphore_signal(barrier, inc=1, device_id={"src": lax.rem(src + r, peers)}, device_id_type=MESH)
        pl.semaphore_signal(barrier, inc=1, device_id={"tgt": lax.rem(tgt + r, peers)}, device_id_type=MESH)

    each_peer(greet)

    def folded(out, rows_of, at, cols):
        wide = cols // LANES
        for w in range(2):
            for k in range(wide):
                out[w * wide + k:w * wide + k + 1, :] = rows_of(w, at + k * LANES)

    def unfolded(ref, at, value):
        wide = value.shape[0] // 2
        for w in range(2):
            for k in range(wide):
                ref[w:w + 1, pl.ds(at + k * LANES, LANES)] = value[w * wide + k:w * wide + k + 1, :]

    def ordered(parts, all_ref, at, cols):
        wide = cols // LANES
        for d in range(peers):
            shuffle[d * 2 * wide:(d + 1) * 2 * wide, :] = parts[d].astype(F32)
        for k in range(wide):
            lanes = at + k * LANES
            all_ref[:, lanes:lanes + LANES] = shuffle[pl.ds(k, weights, stride=wide), :].astype(BF16)

    def scattered(acc, at, cols, out):
        wide = cols // LANES
        for k in range(wide):
            out[pl.ds(k, weights, stride=wide), :] = acc[:, pl.ds(at + k * LANES, LANES)]

    folded(shuffle, lambda w, lane: sc_ref[w:w + 1, lane:lane + LANES], 0, pts)
    u_in[tgt] = shuffle[:u_in.shape[1], :].astype(BF16)
    group = cm_ref[pl.ds(pl.multiple_of(lax.div(src, 4) * 8, 8), 8), :]
    place = lax.rem(src, 4)
    own = jnp.where(place < 2, jnp.where(place == 0, group[0:2], group[2:4]), jnp.where(place == 2, group[4:6], group[6:8]))
    for c in range(CHUNKS):
        folded(col_mass.at[c], lambda w, lane: own[w:w + 1, lane:lane + LANES], c * span, span)
    for c in range(tiles):
        folded(row_mass.at[c], lambda w, lane: rm_ref[w:w + 1, lane:lane + LANES], c * TILE, TILE)

    pl.semaphore_wait(barrier, 2 * (peers - 1))

    def gather_copy(buf, axis, me, r, send, recv):
        return pltpu.make_async_remote_copy(
            src_ref=buf.at[me], dst_ref=buf.at[me], send_sem=send, recv_sem=recv,
            device_id={axis: lax.rem(me + r, peers)}, device_id_type=MESH,
        )

    def group_copy(group, axis, peer, send, recv):
        return pltpu.make_async_remote_copy(
            src_ref=group, dst_ref=group, send_sem=send, recv_sem=recv,
            device_id={axis: peer}, device_id_type=MESH,
        )

    def u_group():
        return group_copy(u_in.at[pl.ds(0, peers - 1)], "tgt", lax.rem(tgt + 1, peers), u_send, u_recv)

    def v_group(c):
        return group_copy(v_in.at[c, pl.ds(0, peers - 1)], "src", lax.rem(src + 1, peers), v_send.at[c], v_recv.at[c])

    def col_group(c):
        return group_copy(col_in.at[c], "src", lax.rem(src + 1, peers), col_send.at[c], col_recv.at[c])

    def row_group(c):
        return group_copy(row_in.at[c], "tgt", xh * half + lax.rem(z + 1, half), row_send.at[c], row_recv.at[c])

    each_peer(lambda r: gather_copy(u_in, "tgt", tgt, r, u_send, u_recv).start())

    def factor_rows(out, parts, own_at, ones_at, own):
        for n, part in enumerate(parts):
            out[3 * n:3 * n + 3, :] = part
        for n, part in enumerate(own):
            out[own_at + n:own_at + n + 1, :] = part
            out[ones_at + n:ones_at + n + 1, :] = jnp.ones_like(part)
        out[30:32, :] = jnp.zeros((2, pts), F32)

    def squares(values):
        return values[0:1] * values[0:1] + values[1:2] * values[1:2] + values[2:3] * values[2:3]

    xc, yc = xc_ref[...] - 0.5, yc_ref[...] - 0.5
    xs, ys = split3((2.0 * RATE) * xc), split3(yc)
    pairs = ((0, 0), (0, 1), (1, 0), (1, 1), (0, 2), (2, 0), (1, 2), (2, 1))
    factor_rows(col_acc, [xs[p] for p, _ in pairs], 24, 27, split3(-RATE * squares(xc)))
    factor_rows(row_acc, [ys[q] for _, q in pairs], 27, 24, split3(math.log2(180.0) - RATE * squares(yc)))

    def rows_at(i):
        return pl.ds(pl.multiple_of(i * TILE, TILE), TILE)

    def lay(i, carry):
        zeros = jnp.zeros((DEPTH - 32, TILE), F32)
        x_fac[rows_at(i), :] = jnp.concatenate([col_acc[0:32, rows_at(i)], zeros], 0).T.astype(BF16)
        y_fac[0:32, rows_at(i)] = row_acc[0:32, rows_at(i)].astype(BF16)
        y_fac[32:, rows_at(i)] = zeros.astype(BF16)
        return carry

    lax.fori_loop(0, tiles, lay, 0)

    def make_piece(start, b, i):
        rows = pl.ds(pl.multiple_of(i * TILE + start, PIECE), PIECE)
        e = jnp.dot(x_fac[rows, :], y_fac[:, rows_at(b)], preferred_element_type=F32)
        return jnp.exp2(e).astype(BF16)

    def make_only(b):
        def step(i, carry):
            e = jnp.dot(x_fac[rows_at(i), :], y_fac[:, b * TILE:(b + 1) * TILE], preferred_element_type=F32)
            near[b - far][rows_at(i), :] = jnp.exp2(e).astype(BF16)
            return carry
        lax.fori_loop(0, tiles, step, 0)

    def use_only(b):
        def step(i, acc):
            return acc + jnp.dot(u_all[:, rows_at(i)], near[b - far][rows_at(i), :], preferred_element_type=F32)
        col_acc[:, b * TILE:(b + 1) * TILE] = lax.fori_loop(0, tiles, step, jnp.zeros((weights, TILE), F32))

    def make_and_use(made, used):
        def step(i, acc):
            for start in range(0, TILE, PIECE):
                rows = pl.ds(pl.multiple_of(i * TILE + start, PIECE), PIECE)
                near[made - far][rows, :] = make_piece(start, made, i)
                acc = acc + jnp.dot(u_all[:, rows], near[used - far][rows, :], preferred_element_type=F32)
            return acc
        col_acc[:, used * TILE:(used + 1) * TILE] = lax.fori_loop(0, tiles, step, jnp.zeros((weights, TILE), F32))

    def stored_copy(slot, t):
        return pltpu.make_async_copy(stage[slot], far_ref.at[lax.div(t, tiles), lax.rem(t, tiles)], stage_sem.at[slot])

    def far_steps(first, last):
        def step(n, carry):
            for slot in range(slots):
                t = n * slots + slot
                b, i = lax.div(t, tiles), lax.rem(t, tiles)
                other = (slot + 1) % slots
                later = jnp.minimum(t + 1, far * tiles - 1)
                lb, li = lax.div(later, tiles), lax.rem(later, tiles)

                @pl.when(t + 1 >= slots)
                def _():
                    stored_copy(other, 0).wait()

                stored_copy(slot, t).start()
                acc = jnp.zeros((weights, TILE), F32)
                for start in range(0, TILE, PIECE):
                    piece = slice(start, start + PIECE)
                    stage[other][piece, :] = make_piece(start, lb, li)
                    rows = pl.ds(pl.multiple_of(i * TILE + start, PIECE), PIECE)
                    acc = acc + jnp.dot(u_all[:, rows], stage[slot][piece, :], preferred_element_type=F32)
                col_acc[:, rows_at(b)] += acc
            return carry
        lax.fori_loop(first // slots, last // slots, step, 0)

    def send_cols(c):
        scattered(col_acc, c * span, span, col_out.at[c])
        rows = 2 * span // LANES

        def send(r):
            peer = lax.rem(src + r, peers)
            pltpu.make_async_remote_copy(
                src_ref=col_out.at[c, pl.ds(pl.multiple_of(peer * rows, rows), rows)], dst_ref=col_in.at[c, r - 1],
                send_sem=col_send.at[c], recv_sem=col_recv.at[c],
                device_id={"src": peer}, device_id_type=MESH,
            ).start()
        each_peer(send)

    def turn_cols(c):
        rows = 2 * span // LANES
        col_group(c).wait_recv()
        value = col_out[c, pl.ds(pl.multiple_of(src * rows, rows), rows)]
        for r in range(peers - 1):
            value = value + col_in[c, r]
        value = col_mass[c] / (value / total)
        v_in[c, src] = value.astype(BF16)
        each_peer(lambda r: gather_copy(v_in.at[c], "src", src, r, v_send.at[c], v_recv.at[c]).start())
        unfolded(tgt_ref, c * span, value)

    def take_cols(c):
        v_group(c).wait_recv()
        ordered(v_in.at[c], v_all, c * span, span)

    make_only(3)
    make_only(4)
    for start in range(0, TILE, PIECE):
        stage[0][start:start + PIECE, :] = make_piece(start, 0, 0)
    u_group().wait_recv()
    ordered(u_in, u_all, 0, pts)
    col_acc[:, :far * TILE] = jnp.zeros((weights, far * TILE), F32)
    far_steps(0, 2 * tiles)
    send_cols(0)
    far_steps(2 * tiles, 3 * tiles)
    make_and_use(5, 3)
    send_cols(1)
    turn_cols(0)
    use_only(4)
    use_only(5)
    send_cols(2)

    count = far * tiles

    def fetch(slot, t):
        return pltpu.make_async_copy(far_ref.at[lax.div(t, tiles), lax.rem(t, tiles)], stage[slot], stage_sem.at[slot])

    def fetch_later(slot, t):
        @pl.when(t < count)
        def _():
            fetch(slot, t).start()

    for slot in range(1, slots):
        stored_copy(slot, 0).wait()
    for t in range(slots):
        fetch(t, t).start()

    def by_rows(b, tile):
        return lax.dot_general(
            v_all[:, b], tile, (((1,), (1,)), ((), ())), preferred_element_type=F32
        )

    def far_rows(first, last, fresh):
        def step(n, carry):
            for slot in range(slots):
                t = n * slots + slot
                i = lax.rem(t, tiles)
                fetch(slot, t).wait()
                part = by_rows(rows_at(lax.div(t, tiles)), stage[slot][...])
                if fresh:
                    row_acc[:, rows_at(i)] = part
                else:
                    row_acc[:, rows_at(i)] += part
                fetch_later(slot, t + slots)
            return carry
        lax.fori_loop(first // slots, last // slots, step, 0)

    def near_rows(b):
        def step(i, carry):
            row_acc[:, rows_at(i)] += by_rows(slice(b * TILE, (b + 1) * TILE), near[b - far][rows_at(i), :])
            return carry
        lax.fori_loop(0, tiles, step, 0)

    own_rows = 2 * TILE // LANES
    half_rows = half * own_rows

    def cross(c):
        return pltpu.make_async_remote_copy(
            src_ref=row_out.at[c, pl.ds(pl.multiple_of((1 - xh) * half_rows, half_rows), half_rows)], dst_ref=row_x.at[c],
            send_sem=x_send.at[c], recv_sem=x_recv.at[c],
            device_id={"tgt": lax.rem(tgt + half, peers)}, device_id_type=MESH,
        )

    def along(c):
        cross(c).wait_recv()
        row_half[c] = row_out[c, pl.ds(pl.multiple_of(xh * half_rows, half_rows), half_rows)] + row_x[c]

        def send(r):
            to = lax.rem(z + r, half)
            pltpu.make_async_remote_copy(
                src_ref=row_half.at[c, pl.ds(pl.multiple_of(to * own_rows, own_rows), own_rows)], dst_ref=row_in.at[c, r - 1],
                send_sem=row_send.at[c], recv_sem=row_recv.at[c],
                device_id={"tgt": xh * half + to}, device_id_type=MESH,
            ).start()
        each_peer(send, half)

    def last_send_all():
        def send(r):
            peer = lax.rem(tgt + r, peers)
            pltpu.make_async_remote_copy(
                src_ref=row_out.at[tiles - 1, pl.ds(pl.multiple_of(peer * own_rows, own_rows), own_rows)],
                dst_ref=last_in.at[r - 1], send_sem=last_send, recv_sem=last_recv,
                device_id={"tgt": peer}, device_id_type=MESH,
            ).start()
        each_peer(send)

    def last_steps(n, carry):
        for slot in range(slots):
            c = n * slots + slot
            part = row_acc[:, rows_at(c)]
            for b in (4, 5):
                part = part + by_rows(slice(b * TILE, (b + 1) * TILE), near[b - far][rows_at(c), :])
            t = 2 * tiles + c
            fetch(slot, t).wait()
            part = part + by_rows(slice(2 * TILE, 3 * TILE), stage[slot][...])
            fetch_later(slot, t + slots)
            row_acc[:, rows_at(c)] = part
            scattered(row_acc, pl.multiple_of(c * TILE, TILE), TILE, row_out.at[c])

            @pl.when(c < tiles - 1)
            def _():
                cross(c).start()

            @pl.when(c == tiles - 1)
            def _():
                last_send_all()

            @pl.when(c > 0)
            def _():
                along(c - 1)
        return carry

    take_cols(0)
    far_rows(0, tiles, True)
    turn_cols(1)
    far_rows(tiles, tiles + slots, False)
    turn_cols(2)
    far_rows(tiles + slots, 2 * tiles, False)
    take_cols(1)
    near_rows(3)
    take_cols(2)
    lax.fori_loop(0, tiles // slots, last_steps, 0)

    def finish(c, carry):
        row_group(c).wait_recv()
        value = row_half[c, pl.ds(pl.multiple_of(z * own_rows, own_rows), own_rows)]
        for r in range(half - 1):
            value = value + row_in[c, r]
        unfolded(new_ref, pl.multiple_of(c * TILE, TILE), row_mass[c] / (value / total))
        row_group(c).wait_send()
        cross(c).wait_send()
        return carry

    lax.fori_loop(0, tiles - 1, finish, 0)
    last = group_copy(last_in, "tgt", lax.rem(tgt + 1, peers), last_send, last_recv)
    last.wait_recv()
    value = row_out[tiles - 1, pl.ds(pl.multiple_of(tgt * own_rows, own_rows), own_rows)]
    for r in range(peers - 1):
        value = value + last_in[r]
    unfolded(new_ref, (tiles - 1) * TILE, row_mass[tiles - 1] / (value / total))
    last.wait_send()
    u_group().wait_send()
    for c in range(CHUNKS):
        col_group(c).wait_send()
        v_group(c).wait_send()


def on_device(src_coords, tgt_coords, src_scaling, src_mass, tgt_mass):
    pts = src_coords.shape[1]
    weights = tgt_mass.shape[0]
    peers = lax.axis_size("src")
    total = float(pts * peers)
    tiles = pts // TILE
    stored = tiles // 2
    span = pts // CHUNKS
    half = peers // 2
    piece, tile_piece = 2 * span // LANES, 2 * TILE // LANES
    vmem = pl.BlockSpec(memory_space=pltpu.VMEM)
    dma = pltpu.SemaphoreType.DMA
    scratch = [
        *[((pts, TILE), BF16)] * stored,
        *[((TILE, TILE), BF16)] * 3,
        ((pts, DEPTH), BF16),
        ((DEPTH, pts), BF16),
        ((peers, 2 * pts // LANES, LANES), BF16),
        ((CHUNKS, peers, piece, LANES), BF16),
        ((weights, pts), BF16),
        ((weights, pts), BF16),
        ((weights * pts // LANES, LANES), F32),
        ((weights, pts), F32),
        ((weights, pts), F32),
        ((CHUNKS, piece, LANES), F32),
        ((tiles, tile_piece, LANES), F32),
        ((CHUNKS, peers * piece, LANES), F32),
        ((CHUNKS, peers - 1, piece, LANES), F32),
        ((tiles, peers * tile_piece, LANES), F32),
        ((tiles, half * tile_piece, LANES), F32),
        ((tiles, half * tile_piece, LANES), F32),
        ((tiles, half - 1, tile_piece, LANES), F32),
        ((peers - 1, tile_piece, LANES), F32),
    ]
    out, _ = pl.pallas_call(
        functools.partial(kernel, total),
        out_shape=(
            jax.ShapeDtypeStruct((2, 2, pts), F32),
            jax.ShapeDtypeStruct((tiles - stored, tiles, TILE, TILE), BF16),
        ),
        in_specs=[vmem] * 5,
        out_specs=(vmem, pl.BlockSpec(memory_space=pl.ANY)),
        scratch_shapes=[pltpu.VMEM(shape, dtype) for shape, dtype in scratch] + [
            dma((3,)), dma, dma, dma((CHUNKS,)), dma((CHUNKS,)), dma((CHUNKS,)), dma((CHUNKS,)),
            dma((tiles,)), dma((tiles,)), dma((tiles,)), dma((tiles,)), dma, dma,
        ],
        compiler_params=pltpu.CompilerParams(
            collective_id=0, has_side_effects=True, vmem_limit_bytes=60 * 2**20
        ),
    )(src_coords, tgt_coords, src_scaling, src_mass, tgt_mass)
    return out[0], out[1]


def solution(mesh):
    placed = (P(None, "src"), P(None, "tgt"), P("tgt", "src"), P("tgt", "src"), P(None, "tgt"))
    return jax.shard_map(
        on_device,
        mesh=mesh,
        in_specs=placed,
        out_specs=(P("tgt", "src"), P("src", "tgt")),
        check_vma=False,
    )
```

```python
import functools
import math

import jax
import jax.numpy as jnp
from jax import lax
from jax.experimental import pallas as pl
from jax.experimental.pallas import tpu as pltpu
from jax.sharding import PartitionSpec as P

F32, BF16 = jnp.float32, jnp.bfloat16
MESH = pl.DeviceIdType.MESH
RATE = 100.0 / math.log(2.0)
TILE = 1024
PIECE = 256
CHUNKS = 3
DEPTH = 128
LANES = 128


def split3(values):
    first = values.astype(BF16).astype(F32)
    rest = values - first
    second = rest.astype(BF16).astype(F32)
    return first, second, rest - second


def kernel(
    total, xc_ref, yc_ref, sc_ref, rm_ref, cm_ref,
    out_ref, far_ref,
    near0, near1, near2, stage0, stage1, stage2, x_fac, y_fac, u_in, v_in, u_all, v_all, shuffle, col_acc, row_acc, col_mass, row_mass,
    col_out, col_in, row_out, row_x, row_half, row_in, last_in,
    stage_sem, u_send, u_recv, v_send, v_recv, col_send, col_recv, x_send, x_recv, row_send, row_recv, last_send, last_recv,
):
    src, tgt = lax.axis_index("src"), lax.axis_index("tgt")
    peers = lax.axis_size("src")
    weights = 2 * peers
    pts = sc_ref.shape[1]
    blocks = tiles = pts // TILE
    new_ref, tgt_ref = out_ref.at[0], out_ref.at[1]
    near, stage = (near0, near1, near2), (stage0, stage1, stage2)
    slots, far = len(stage), blocks - len(near)
    span = pts // CHUNKS
    half = peers // 2
    xh, z = lax.div(tgt, half), lax.rem(tgt, half)

    def each_peer(body, count=peers):
        def step(r, carry):
            body(r)
            return carry
        lax.fori_loop(1, count, step, 0)

    barrier = pltpu.get_barrier_semaphore()

    def greet(r):
        pl.semaphore_signal(barrier, inc=1, device_id={"src": lax.rem(src + r, peers)}, device_id_type=MESH)
        pl.semaphore_signal(barrier, inc=1, device_id={"tgt": lax.rem(tgt + r, peers)}, device_id_type=MESH)

    each_peer(greet)

    def folded(out, rows_of, at, cols):
        wide = cols // LANES
        for w in range(2):
            for k in range(wide):
                out[w * wide + k:w * wide + k + 1, :] = rows_of(w, at + k * LANES)

    def unfolded(ref, at, value):
        wide = value.shape[0] // 2
        for w in range(2):
            for k in range(wide):
                ref[w:w + 1, pl.ds(at + k * LANES, LANES)] = value[w * wide + k:w * wide + k + 1, :]

    def ordered(parts, all_ref, at, cols):
        wide = cols // LANES
        for d in range(peers):
            shuffle[d * 2 * wide:(d + 1) * 2 * wide, :] = parts[d].astype(F32)
        for k in range(wide):
            lanes = at + k * LANES
            all_ref[:, lanes:lanes + LANES] = shuffle[pl.ds(k, weights, stride=wide), :].astype(BF16)

    def scattered(acc, at, cols, out):
        wide = cols // LANES
        for k in range(wide):
            out[pl.ds(k, weights, stride=wide), :] = acc[:, pl.ds(at + k * LANES, LANES)]

    folded(shuffle, lambda w, lane: sc_ref[w:w + 1, lane:lane + LANES], 0, pts)
    u_in[tgt] = shuffle[:u_in.shape[1], :].astype(BF16)
    group = cm_ref[pl.ds(pl.multiple_of(lax.div(src, 4) * 8, 8), 8), :]
    place = lax.rem(src, 4)
    own = jnp.where(place < 2, jnp.where(place == 0, group[0:2], group[2:4]), jnp.where(place == 2, group[4:6], group[6:8]))
    for c in range(CHUNKS):
        folded(col_mass.at[c], lambda w, lane: own[w:w + 1, lane:lane + LANES], c * span, span)
    for c in range(tiles):
        folded(row_mass.at[c], lambda w, lane: rm_ref[w:w + 1, lane:lane + LANES], c * TILE, TILE)

    pl.semaphore_wait(barrier, 2 * (peers - 1))

    def gather_copy(buf, axis, me, r, send, recv):
        return pltpu.make_async_remote_copy(
            src_ref=buf.at[me], dst_ref=buf.at[me], send_sem=send, recv_sem=recv,
            device_id={axis: lax.rem(me + r, peers)}, device_id_type=MESH,
        )

    def group_copy(group, axis, peer, send, recv):
        return pltpu.make_async_remote_copy(
            src_ref=group, dst_ref=group, send_sem=send, recv_sem=recv,
            device_id={axis: peer}, device_id_type=MESH,
        )

    def u_group():
        return group_copy(u_in.at[pl.ds(0, peers - 1)], "tgt", lax.rem(tgt + 1, peers), u_send, u_recv)

    def v_group(c):
        return group_copy(v_in.at[c, pl.ds(0, peers - 1)], "src", lax.rem(src + 1, peers), v_send.at[c], v_recv.at[c])

    def col_group(c):
        return group_copy(col_in.at[c], "src", lax.rem(src + 1, peers), col_send.at[c], col_recv.at[c])

    def row_group(c):
        return group_copy(row_in.at[c], "tgt", xh * half + lax.rem(z + 1, half), row_send.at[c], row_recv.at[c])

    each_peer(lambda r: gather_copy(u_in, "tgt", tgt, r, u_send, u_recv).start())

    def factor_rows(out, parts, own_at, ones_at, own):
        for n, part in enumerate(parts):
            out[3 * n:3 * n + 3, :] = part
        for n, part in enumerate(own):
            out[own_at + n:own_at + n + 1, :] = part
            out[ones_at + n:ones_at + n + 1, :] = jnp.ones_like(part)
        out[30:32, :] = jnp.zeros((2, pts), F32)

    def squares(values):
        return values[0:1] * values[0:1] + values[1:2] * values[1:2] + values[2:3] * values[2:3]

    xc, yc = xc_ref[...] - 0.5, yc_ref[...] - 0.5
    xs, ys = split3((2.0 * RATE) * xc), split3(yc)
    pairs = ((0, 0), (0, 1), (1, 0), (1, 1), (0, 2), (2, 0), (1, 2), (2, 1))
    factor_rows(col_acc, [xs[p] for p, _ in pairs], 24, 27, split3(-RATE * squares(xc)))
    factor_rows(row_acc, [ys[q] for _, q in pairs], 27, 24, split3(math.log2(180.0) - RATE * squares(yc)))

    def rows_at(i):
        return pl.ds(pl.multiple_of(i * TILE, TILE), TILE)

    def lay(i, carry):
        zeros = jnp.zeros((DEPTH - 32, TILE), F32)
        x_fac[rows_at(i), :] = jnp.concatenate([col_acc[0:32, rows_at(i)], zeros], 0).T.astype(BF16)
        y_fac[0:32, rows_at(i)] = row_acc[0:32, rows_at(i)].astype(BF16)
        y_fac[32:, rows_at(i)] = zeros.astype(BF16)
        return carry

    lax.fori_loop(0, tiles, lay, 0)

    def make_piece(start, b, i):
        rows = pl.ds(pl.multiple_of(i * TILE + start, PIECE), PIECE)
        e = jnp.dot(x_fac[rows, :], y_fac[:, rows_at(b)], preferred_element_type=F32)
        return jnp.exp2(e).astype(BF16)

    def make_only(b):
        def step(i, carry):
            e = jnp.dot(x_fac[rows_at(i), :], y_fac[:, b * TILE:(b + 1) * TILE], preferred_element_type=F32)
            near[b - far][rows_at(i), :] = jnp.exp2(e).astype(BF16)
            return carry
        lax.fori_loop(0, tiles, step, 0)

    def use_only(b):
        def step(i, acc):
            return acc + jnp.dot(u_all[:, rows_at(i)], near[b - far][rows_at(i), :], preferred_element_type=F32)
        col_acc[:, b * TILE:(b + 1) * TILE] = lax.fori_loop(0, tiles, step, jnp.zeros((weights, TILE), F32), unroll=3)

    def make_and_use(made, used):
        def step(i, acc):
            for start in range(0, TILE, PIECE):
                rows = pl.ds(pl.multiple_of(i * TILE + start, PIECE), PIECE)
                near[made - far][rows, :] = make_piece(start, made, i)
                acc = acc + jnp.dot(u_all[:, rows], near[used - far][rows, :], preferred_element_type=F32)
            return acc
        col_acc[:, used * TILE:(used + 1) * TILE] = lax.fori_loop(0, tiles, step, jnp.zeros((weights, TILE), F32))

    def stored_copy(slot, t):
        return pltpu.make_async_copy(stage[slot], far_ref.at[lax.div(t, tiles), lax.rem(t, tiles)], stage_sem.at[slot])

    def far_steps(first, last):
        def step(n, carry):
            for slot in range(slots):
                t = n * slots + slot
                b, i = lax.div(t, tiles), lax.rem(t, tiles)
                other = (slot + 1) % slots
                later = jnp.minimum(t + 1, far * tiles - 1)
                lb, li = lax.div(later, tiles), lax.rem(later, tiles)

                @pl.when(t + 1 >= slots)
                def _():
                    stored_copy(other, 0).wait()

                stored_copy(slot, t).start()
                acc = jnp.zeros((weights, TILE), F32)
                for start in range(0, TILE, PIECE):
                    piece = slice(start, start + PIECE)
                    stage[other][piece, :] = make_piece(start, lb, li)
                    rows = pl.ds(pl.multiple_of(i * TILE + start, PIECE), PIECE)
                    acc = acc + jnp.dot(u_all[:, rows], stage[slot][piece, :], preferred_element_type=F32)
                col_acc[:, rows_at(b)] += acc
            return carry
        lax.fori_loop(first // slots, last // slots, step, 0)

    def send_cols(c):
        scattered(col_acc, c * span, span, col_out.at[c])
        rows = 2 * span // LANES

        def send(r):
            peer = lax.rem(src + r, peers)
            pltpu.make_async_remote_copy(
                src_ref=col_out.at[c, pl.ds(pl.multiple_of(peer * rows, rows), rows)], dst_ref=col_in.at[c, r - 1],
                send_sem=col_send.at[c], recv_sem=col_recv.at[c],
                device_id={"src": peer}, device_id_type=MESH,
            ).start()
        each_peer(send)

    def turn_cols(c):
        rows = 2 * span // LANES
        col_group(c).wait_recv()
        value = col_out[c, pl.ds(pl.multiple_of(src * rows, rows), rows)]
        for r in range(peers - 1):
            value = value + col_in[c, r]
        value = col_mass[c] / (value / total)
        v_in[c, src] = value.astype(BF16)
        each_peer(lambda r: gather_copy(v_in.at[c], "src", src, r, v_send.at[c], v_recv.at[c]).start())
        unfolded(tgt_ref, c * span, value)

    def take_cols(c):
        v_group(c).wait_recv()
        ordered(v_in.at[c], v_all, c * span, span)

    make_only(3)
    make_only(4)
    for start in range(0, TILE, PIECE):
        stage[0][start:start + PIECE, :] = make_piece(start, 0, 0)
    u_group().wait_recv()
    ordered(u_in, u_all, 0, pts)
    col_acc[:, :far * TILE] = jnp.zeros((weights, far * TILE), F32)
    far_steps(0, 2 * tiles)
    send_cols(0)
    far_steps(2 * tiles, 3 * tiles)
    make_and_use(5, 3)
    send_cols(1)
    turn_cols(0)
    use_only(4)
    use_only(5)
    send_cols(2)

    count = far * tiles

    def fetch(slot, t):
        return pltpu.make_async_copy(far_ref.at[lax.div(t, tiles), lax.rem(t, tiles)], stage[slot], stage_sem.at[slot])

    def fetch_later(slot, t):
        @pl.when(t < count)
        def _():
            fetch(slot, t).start()

    for slot in range(1, slots):
        stored_copy(slot, 0).wait()
    for t in range(slots):
        fetch(t, t).start()

    def by_rows(b, tile):
        return lax.dot_general(
            v_all[:, b], tile, (((1,), (1,)), ((), ())), preferred_element_type=F32
        )

    def far_rows(b, first, last, fresh):
        def step(n, carry):
            for slot in range(slots):
                t = n * slots + slot
                i = lax.rem(t, tiles)
                fetch(slot, t).wait()
                part = by_rows(slice(b * TILE, (b + 1) * TILE), stage[slot][...])
                if fresh:
                    row_acc[:, rows_at(i)] = part
                else:
                    row_acc[:, rows_at(i)] += part
                fetch_later(slot, t + slots)
            return carry
        lax.fori_loop(first // slots, last // slots, step, 0)

    def near_rows(b):
        def step(i, carry):
            row_acc[:, rows_at(i)] += by_rows(slice(b * TILE, (b + 1) * TILE), near[b - far][rows_at(i), :])
            return carry
        lax.fori_loop(0, tiles, step, 0, unroll=3)

    own_rows = 2 * TILE // LANES
    half_rows = half * own_rows

    def cross(c):
        return pltpu.make_async_remote_copy(
            src_ref=row_out.at[c, pl.ds(pl.multiple_of((1 - xh) * half_rows, half_rows), half_rows)], dst_ref=row_x.at[c],
            send_sem=x_send.at[c], recv_sem=x_recv.at[c],
            device_id={"tgt": lax.rem(tgt + half, peers)}, device_id_type=MESH,
        )

    def along(c):
        cross(c).wait_recv()
        row_half[c] = row_out[c, pl.ds(pl.multiple_of(xh * half_rows, half_rows), half_rows)] + row_x[c]

        def send(r):
            to = lax.rem(z + r, half)
            pltpu.make_async_remote_copy(
                src_ref=row_half.at[c, pl.ds(pl.multiple_of(to * own_rows, own_rows), own_rows)], dst_ref=row_in.at[c, r - 1],
                send_sem=row_send.at[c], recv_sem=row_recv.at[c],
                device_id={"tgt": xh * half + to}, device_id_type=MESH,
            ).start()
        each_peer(send, half)

    def last_send_all():
        def send(r):
            peer = lax.rem(tgt + r, peers)
            pltpu.make_async_remote_copy(
                src_ref=row_out.at[tiles - 1, pl.ds(pl.multiple_of(peer * own_rows, own_rows), own_rows)],
                dst_ref=last_in.at[r - 1], send_sem=last_send, recv_sem=last_recv,
                device_id={"tgt": peer}, device_id_type=MESH,
            ).start()
        each_peer(send)

    def last_steps(n, carry):
        for slot in range(slots):
            c = n * slots + slot
            part = row_acc[:, rows_at(c)]
            for b in (4, 5):
                part = part + by_rows(slice(b * TILE, (b + 1) * TILE), near[b - far][rows_at(c), :])
            t = 2 * tiles + c
            fetch(slot, t).wait()
            part = part + by_rows(slice(2 * TILE, 3 * TILE), stage[slot][...])
            fetch_later(slot, t + slots)
            row_acc[:, rows_at(c)] = part
            scattered(row_acc, pl.multiple_of(c * TILE, TILE), TILE, row_out.at[c])

            @pl.when(c < tiles - 1)
            def _():
                cross(c).start()

            @pl.when(c == tiles - 1)
            def _():
                last_send_all()

            @pl.when(c > 0)
            def _():
                along(c - 1)
        return carry

    take_cols(0)
    far_rows(0, 0, tiles, True)
    turn_cols(1)
    far_rows(1, tiles, tiles + slots, False)
    turn_cols(2)
    far_rows(1, tiles + slots, 2 * tiles, False)
    take_cols(1)
    near_rows(3)
    take_cols(2)
    lax.fori_loop(0, tiles // slots, last_steps, 0)

    def finish(c, carry):
        row_group(c).wait_recv()
        value = row_half[c, pl.ds(pl.multiple_of(z * own_rows, own_rows), own_rows)]
        for r in range(half - 1):
            value = value + row_in[c, r]
        unfolded(new_ref, pl.multiple_of(c * TILE, TILE), row_mass[c] / (value / total))
        row_group(c).wait_send()
        cross(c).wait_send()
        return carry

    lax.fori_loop(0, tiles - 1, finish, 0)
    last = group_copy(last_in, "tgt", lax.rem(tgt + 1, peers), last_send, last_recv)
    last.wait_recv()
    value = row_out[tiles - 1, pl.ds(pl.multiple_of(tgt * own_rows, own_rows), own_rows)]
    for r in range(peers - 1):
        value = value + last_in[r]
    unfolded(new_ref, (tiles - 1) * TILE, row_mass[tiles - 1] / (value / total))
    last.wait_send()
    u_group().wait_send()
    for c in range(CHUNKS):
        col_group(c).wait_send()
        v_group(c).wait_send()


def on_device(src_coords, tgt_coords, src_scaling, src_mass, tgt_mass):
    pts = src_coords.shape[1]
    weights = tgt_mass.shape[0]
    peers = lax.axis_size("src")
    total = float(pts * peers)
    tiles = pts // TILE
    stored = tiles // 2
    span = pts // CHUNKS
    half = peers // 2
    piece, tile_piece = 2 * span // LANES, 2 * TILE // LANES
    vmem = pl.BlockSpec(memory_space=pltpu.VMEM)
    dma = pltpu.SemaphoreType.DMA
    scratch = [
        *[((pts, TILE), BF16)] * stored,
        *[((TILE, TILE), BF16)] * 3,
        ((pts, DEPTH), BF16),
        ((DEPTH, pts), BF16),
        ((peers, 2 * pts // LANES, LANES), BF16),
        ((CHUNKS, peers, piece, LANES), BF16),
        ((weights, pts), BF16),
        ((weights, pts), BF16),
        ((weights * pts // LANES, LANES), F32),
        ((weights, pts), F32),
        ((weights, pts), F32),
        ((CHUNKS, piece, LANES), F32),
        ((tiles, tile_piece, LANES), F32),
        ((CHUNKS, peers * piece, LANES), F32),
        ((CHUNKS, peers - 1, piece, LANES), F32),
        ((tiles, peers * tile_piece, LANES), F32),
        ((tiles, half * tile_piece, LANES), F32),
        ((tiles, half * tile_piece, LANES), F32),
        ((tiles, half - 1, tile_piece, LANES), F32),
        ((peers - 1, tile_piece, LANES), F32),
    ]
    out, _ = pl.pallas_call(
        functools.partial(kernel, total),
        out_shape=(
            jax.ShapeDtypeStruct((2, 2, pts), F32),
            jax.ShapeDtypeStruct((tiles - stored, tiles, TILE, TILE), BF16),
        ),
        in_specs=[vmem] * 5,
        out_specs=(vmem, pl.BlockSpec(memory_space=pl.ANY)),
        scratch_shapes=[pltpu.VMEM(shape, dtype) for shape, dtype in scratch] + [
            dma((3,)), dma, dma, dma((CHUNKS,)), dma((CHUNKS,)), dma((CHUNKS,)), dma((CHUNKS,)),
            dma((tiles,)), dma((tiles,)), dma((tiles,)), dma((tiles,)), dma, dma,
        ],
        compiler_params=pltpu.CompilerParams(
            collective_id=0, has_side_effects=True, vmem_limit_bytes=60 * 2**20
        ),
    )(src_coords, tgt_coords, src_scaling, src_mass, tgt_mass)
    return out[0], out[1]


def solution(mesh):
    placed = (P(None, "src"), P(None, "tgt"), P("tgt", "src"), P("tgt", "src"), P(None, "tgt"))
    return jax.shard_map(
        on_device,
        mesh=mesh,
        in_specs=placed,
        out_specs=(P("tgt", "src"), P("src", "tgt")),
        check_vma=False,
    )
```
